512 devices in a mesh: row: 16 (over x, y_hi, core), col: 16 (over z), atom: 2 (over y_lo).
Axes of the slice: x: 4, y: 4 (y_hi: 2, y_lo: 2; y = y_hi * 2 + y_lo), z: 16, core: 2. Of those that a mesh axis runs over, the one named last changes fastest.
Arguments:
- proj: bfloat16 [24, 104, 12288], P('atom', None, 'row'), may hold values from -1.5 to 1.5
- nbr: int32 [24, 96], P('atom', 'row'), may hold values from -1 to 117, as said below
- dh: float32 [118, 8, 13, 13], P('atom'), may hold values from -1 to 1, as said below
Outputs:
- correction: float32 [12288, 12288], P('row', ('col', 'atom'))
The draws below stay inside these ranges and needn't reach their ends.
Inputs may be any that keep to these rules, and one draw needn't show every extreme that they name: `nbr`: rows s * 12 to (s + 1) * 12 - 1 hold, for each basis tile, its neighbours among atom tiles s * 59 to (s + 1) * 59 - 1: live entries first, distinct and rising, then -1 in empty slots; every list has at least 6 live entries, and in every subset some list has all 12 live. dh[A, a] is symmetric.
All inputs are finite; a program needn't handle non-finite values.
Results may differ from the reference program's by a relative error of at most 0.0029.
Values may be sent and summed in bfloat16 or wider, within the bound.
A program may use at most 64 MiB of HBM per device.

```python
import jax
import jax.numpy as jnp
from jax import lax

BT = 128
NPJ = 13
ATB = 8
AP = 104
NBT = 96
NB = 12288
NATS = 59
NAT = 118
LS = 12
N_ATOM = 2


def live_counts(key):
    key = jax.random.fold_in(key, 11)
    counts = jax.random.randint(key, (N_ATOM, NBT), (LS + 1) // 2, LS + 1)
    place = jax.random.randint(jax.random.fold_in(key, 1), (N_ATOM,), 0, NBT)
    return jnp.where(jnp.arange(NBT)[None, :] == place[:, None], LS, counts)


def draw_nbr(key, part):
    counts = live_counts(key)
    key = jax.random.fold_in(key, 3)
    scores = jax.random.randint(key, (N_ATOM, NBT, NATS), 0, 1 << 16) * NATS + jnp.arange(NATS)[None, None, :]
    order = jnp.argsort(scores, axis=-1, stable=True)
    picked = jnp.sort(order[:, :, :LS], axis=-1)
    picked = picked + (jnp.arange(N_ATOM) * NATS)[:, None, None]
    slots = jnp.arange(LS)[None, None, :]
    picked = jnp.where(slots < counts[:, :, None], picked, -1)
    return jnp.transpose(picked, (0, 2, 1)).reshape(N_ATOM * LS, NBT).astype(jnp.int32)


def draw_proj(key, part):
    key = jax.random.fold_in(key, 5)
    values = jnp.clip(0.25 * jax.random.normal(key, (N_ATOM, LS, AP, NBT, BT), jnp.float32), -1.5, 1.5)
    return values.reshape(N_ATOM * LS, AP, NB).astype(jnp.bfloat16)


def draw_dh(key, part):
    key = jax.random.fold_in(key, 7)
    base = jax.random.normal(key, (NAT, ATB, NPJ, NPJ), jnp.float32)
    sym = (base + jnp.swapaxes(base, -1, -2)) * 0.5 ** 0.5 / NPJ ** 0.5
    return jnp.clip(sym, -1.0, 1.0)


def setup_inputs(seed: int = 0) -> dict:
    seeds = jax.random.split(jax.random.key(seed), 4)
    return {
        "proj": draw_proj(jax.random.fold_in(seeds[3], 71), 0),
        "nbr": draw_nbr(jax.random.fold_in(seeds[3], 71), 0),
        "dh": draw_dh(jax.random.fold_in(seeds[3], 71), 0),
    }


def form_products(blockp, blockid, table, base):
    lcount, ap, rows = blockp.shape
    tiles = blockid.shape[1]
    width = rows // tiles
    natoms, atb, npj, unused = table.shape
    safe = jnp.clip(blockid - base, 0, natoms - 1).astype(jnp.int32)
    chosen = table[safe]
    ptile = blockp.reshape(lcount, atb, npj, tiles, width).astype(jnp.float32)
    prod = jnp.einsum('ltaij,lajtb->laitb', chosen, ptile, precision=lax.Precision.HIGHEST)
    return prod.reshape(lcount, ap, rows).astype(jnp.bfloat16)


def assemble(rowp, rowid, colq, colid):
    lcount, ap, rows = rowp.shape
    rtiles = rowid.shape[1]
    width = rows // rtiles
    ctiles = colid.shape[1]
    mcount = colq.shape[0]
    ptile = rowp.reshape(lcount, ap, rtiles, width).astype(jnp.float32)
    qtile = jnp.moveaxis(colq.reshape(mcount, ap, ctiles, width), 2, 0)
    idtile = jnp.moveaxis(colid, 1, 0)

    def one_tile(args):
        qpiece, idpiece = args
        match = (jnp.transpose(rowid)[:, :, None] == idpiece[None, None, :]) & (idpiece[None, None, :] >= 0)
        match = match.astype(jnp.float32)
        picked = jnp.einsum('tlm,mpb->tlpb', match, qpiece.astype(jnp.float32))
        return jnp.einsum('lptx,tlpb->txb', ptile, picked)

    blocks = lax.map(one_tile, (qtile, idtile))
    return jnp.transpose(blocks, (1, 2, 0, 3)).reshape(rows, ctiles * width)


def reference(proj, nbr, dh):
    products = form_products(proj, nbr, dh, 0)
    return assemble(proj, nbr, products, nbr)
```

```python
import functools

import jax
import jax.numpy as jnp
from jax import lax
from jax.experimental import pallas as pl
from jax.experimental.pallas import tpu as pltpu
from jax.sharding import PartitionSpec as P

MESH = pl.DeviceIdType.MESH
BT = 128
PAD = 16


def kernel(proj, dh, ids, out, pbuf, colb, dhv, xpad, dhi, dlo, pt, sel, q, acc, xsend, xrecv,
           colx, idv, ids_s, lsem, dsem, isem, nsend, nrecv, rsem, ssem, xssem, xrsem):
    slots, ap, _ = proj.shape
    nats, atb, npj, _ = dh.shape
    tiles = pbuf.shape[0]
    half = tiles // 2
    part = slots // 4
    row, c, a = lax.axis_index("row"), lax.axis_index("col"), lax.axis_index("atom")
    x, h, k = row // 4, (row // 2) % 2, row % 2
    xs, hs, ks = c // 4, (c // 2) % 2, c % 2
    is_root = row == c
    root_chip = (row // 2) == (c // 2)

    def dev(x_, h_, k_):
        return (x_ * 4 + h_ * 2 + k_, c, a)

    def tile_of(t):
        return (t + half * (1 - a)) % tiles

    bar = pltpu.get_barrier_semaphore()
    for i in range(1, 16):
        pl.semaphore_signal(bar, inc=1, device_id=((row + i) % 16, c, a), device_id_type=MESH)
    pl.semaphore_signal(bar, inc=1, device_id=(row, c, 1 - a), device_id_type=MESH)

    loads = [
        pltpu.make_async_copy(proj.at[:, :, pl.ds(i * BT, BT)], pbuf.at[i], lsem.at[i])
        for i in range(tiles)
    ]
    for cp in loads:
        cp.start()
    dcopy = pltpu.make_async_copy(dh, dhv, dsem)
    dcopy.start()
    for cp in loads:
        cp.wait()
    pl.semaphore_wait(bar, 16)

    def quarter(buf, t, qx):
        return buf.at[t, pl.ds(part * qx, part)]

    def send(src, t, qx, slot, target):
        return pltpu.make_async_remote_copy(
            src_ref=src, dst_ref=quarter(colb, t, qx), send_sem=ssem.at[t, slot],
            recv_sem=rsem.at[t, qx], device_id=target, device_id_type=MESH)

    def root_ids(i):
        return pltpu.make_async_remote_copy(
            src_ref=ids.at[pl.ds(16, 16)], dst_ref=colx, send_sem=nsend.at[i - 1],
            recv_sem=nrecv, device_id=((row + i) % 16, c, a), device_id_type=MESH)

    def root_sends(t):
        kt = t % 2
        tile = tile_of(t)
        own = quarter(pbuf, tile, xs)
        copies = []
        for n, d in enumerate((1, 3, 2)):
            qx = (xs + d) % 4
            copies.append(send(quarter(pbuf, tile, qx), t, qx, n, dev(qx, hs, kt)))
        copies.append(send(own, t, xs, 3, dev(xs, 1 - hs, kt)))
        for n, d in enumerate((1, 3, 2)):
            copies.append(send(own, t, xs, 4 + n, dev((xs + d) % 4, hs, kt)))
        for qx in range(4):
            copies.append(send(quarter(pbuf, tile, qx), t, qx, 7 + qx, dev(xs, hs, 1 - ks)))
        return copies

    @pl.when(is_root)
    def _():
        for i in range(1, 16):
            root_ids(i).start()
        pltpu.make_async_copy(ids.at[pl.ds(16, 16)], colx, nrecv).start()

        def step(t, carry):
            for cp in root_sends(t):
                cp.start()
            for qx in range(4):
                pltpu.make_async_copy(
                    quarter(pbuf, tile_of(t), qx), quarter(colb, t, qx), rsem.at[t, qx]).start()
            return carry

        lax.fori_loop(0, tiles, step, 0)

    def arrived(t, qx):
        pltpu.make_async_copy(quarter(colb, t, qx), quarter(colb, t, qx), rsem.at[t, qx]).wait()

    def relay(t):
        return (k == t % 2) & jnp.logical_not(root_chip)

    def relay_first(t):
        mine = quarter(colb, t, x)
        cross = send(mine, t, x, 0, dev(x, 1 - hs, k))
        along = [(send(mine, t, x, 1 + n, dev((x + d) % 4, h, k)),
                  jnp.logical_not((h == hs) & ((x + d) % 4 == xs)))
                 for n, d in enumerate((1, 3, 2))]
        twin = send(mine, t, x, 4, dev(x, h, 1 - k))
        return cross, along, twin

    def relay_rest(t):
        return [((x + d) % 4, send(quarter(colb, t, (x + d) % 4), t, (x + d) % 4, 5 + n,
                                   dev(x, h, 1 - k)))
                for n, d in enumerate((1, 3, 2))]

    def forward_first(t):
        @pl.when(relay(t))
        def _():
            arrived(t, x)
            cross, along, twin = relay_first(t)

            @pl.when(h == hs)
            def _():
                cross.start()

            for cp, needed in along:
                @pl.when(needed)
                def _():
                    cp.start()

            twin.start()

    def forward_rest(t):
        @pl.when(relay(t))
        def _():
            for qx, cp in relay_rest(t):
                arrived(t, qx)
                cp.start()

        @pl.when(jnp.logical_not(relay(t)))
        def _():
            for qx in range(4):
                arrived(t, qx)

    dcopy.wait()
    xpad[...] = jnp.zeros_like(xpad)

    def table(i, carry):
        xpad[:, 0:npj, 0:npj] = dhv[i]
        for b in range(atb):
            v = xpad[b]
            if b:
                v = pltpu.roll(v, npj * b, 1)
            hi = v.astype(jnp.bfloat16)
            dhi[i, b * PAD:(b + 1) * PAD, :] = hi
            dlo[i, b * PAD:(b + 1) * PAD, :] = (v - hi.astype(jnp.float32)).astype(jnp.bfloat16)
        return carry

    lax.fori_loop(0, nats, table, 0)

    forward_first(0)
    forward_first(1)

    pidx = lax.broadcasted_iota(jnp.int32, (ap, BT), 0)
    sidx = lax.broadcasted_iota(jnp.int32, (ap, BT), 1)
    spread = ((sidx >> 4) * npj + (sidx & 15) == pidx) & ((sidx & 15) < npj)
    spread = spread.astype(jnp.float32).astype(jnp.bfloat16)

    def flip(u, carry):
        for l in range(slots):
            pt[u, l] = lax.dot_general(
                pbuf[u, l], spread, (((0,), (0,)), ((), ())),
                preferred_element_type=jnp.float32).astype(jnp.bfloat16)
        pt[u, slots] = jnp.zeros((BT, BT), jnp.bfloat16)
        return carry

    lax.fori_loop(0, tiles, flip, 0)

    pltpu.make_async_copy(ids.at[pl.ds(16, 16)], colx, nrecv).wait()
    cols = colx[...]
    found = jnp.full((16, BT), slots, jnp.int32)
    for l in range(slots):
        same = (ids[l:l + 1, :] == cols) & (cols >= 0)
        found = jnp.where(same, l, found)
    idv[0:16, :] = found
    idv[16:32, :] = jnp.clip(cols - a * nats, 0, nats - 1)
    icopy = pltpu.make_async_copy(idv, ids_s, isem)
    icopy.start()
    icopy.wait()

    def exchange(t):
        return pltpu.make_async_remote_copy(
            src_ref=xsend.at[t], dst_ref=xrecv.at[t], send_sem=xssem.at[t], recv_sem=xrsem.at[t],
            device_id=(row, c, 1 - a), device_id_type=MESH)

    def step(t, carry):
        @pl.when(t + 2 < tiles)
        def _():
            forward_first(t + 2)

        forward_rest(t)
        tile = tile_of(t)
        for m in range(slots):
            i = ids_s[16 + m, tile * tiles]
            piece = colb[t, m]
            prod = jnp.dot(dhi[i][:, :ap], piece, preferred_element_type=jnp.float32)
            prod += jnp.dot(dlo[i][:, :ap], piece, preferred_element_type=jnp.float32)
            q[m * BT:(m + 1) * BT, :] = prod.astype(jnp.bfloat16)
        for u in range(tiles):
            for m in range(slots):
                l = ids_s[m, tile * tiles + u]
                sel[u * BT:(u + 1) * BT, m * BT:(m + 1) * BT] = pt[u, l]
        block = jnp.dot(sel[...], q[...], preferred_element_type=jnp.float32)

        @pl.when(t < half)
        def _():
            xsend[t] = block.astype(jnp.bfloat16)
            exchange(t).start()

        @pl.when(t >= half)
        def _():
            acc[t - half] = block

        return carry

    lax.fori_loop(0, tiles, step, 0)

    for j in range(half):
        exchange(j).wait_recv()
        out[:, j * BT:(j + 1) * BT] = acc[j] + xrecv[j].astype(jnp.float32)

    for j in range(half):
        exchange(j).wait_send()

    @pl.when(is_root)
    def _():
        for i in range(1, 16):
            root_ids(i).wait_send()

        def drain(t, carry):
            for cp in root_sends(t):
                cp.wait_send()
            return carry

        lax.fori_loop(0, tiles, drain, 0)

    def drain(t, carry):
        @pl.when(relay(t))
        def _():
            cross, along, twin = relay_first(t)

            @pl.when(h == hs)
            def _():
                cross.wait_send()

            for cp, needed in along:
                @pl.when(needed)
                def _():
                    cp.wait_send()

            twin.wait_send()
            for _, cp in relay_rest(t):
                cp.wait_send()

        return carry

    lax.fori_loop(0, tiles, drain, 0)


def on_device(proj, nbr, dh):
    slots, ap, rows = proj.shape
    tiles = nbr.shape[1]
    nats, atb, npj, _ = dh.shape
    half = tiles // 2
    rowx = jnp.tile(nbr, (1, tiles))
    colx = jnp.repeat(nbr, tiles, axis=1)
    pad = ((0, 16 - slots), (0, BT - tiles * tiles))
    ids = jnp.concatenate([jnp.pad(v, pad, constant_values=-1) for v in (rowx, colx)], axis=0)
    bf, f32 = jnp.bfloat16, jnp.float32
    return pl.pallas_call(
        kernel,
        out_shape=jax.ShapeDtypeStruct((rows, half * BT), f32),
        in_specs=[pl.BlockSpec(memory_space=pl.ANY), pl.BlockSpec(memory_space=pl.ANY),
                  pl.BlockSpec(memory_space=pltpu.VMEM)],
        out_specs=pl.BlockSpec(memory_space=pltpu.VMEM),
        scratch_shapes=[
            pltpu.VMEM((tiles, slots, ap, BT), bf),
            pltpu.VMEM((tiles, slots, ap, BT), bf),
            pltpu.VMEM(dh.shape, f32),
            pltpu.VMEM((atb, PAD, BT), f32),
            pltpu.VMEM((nats, atb * PAD, BT), bf),
            pltpu.VMEM((nats, atb * PAD, BT), bf),
            pltpu.VMEM((tiles, slots + 1, BT, BT), bf),
            pltpu.VMEM((rows, slots * BT), bf),
            pltpu.VMEM((slots * BT, BT), bf),
            pltpu.VMEM((half, rows, BT), f32),
            pltpu.VMEM((half, rows, BT), bf),
            pltpu.VMEM((half, rows, BT), bf),
            pltpu.VMEM((16, BT), jnp.int32),
            pltpu.VMEM((32, BT), jnp.int32),
            pltpu.SMEM((32, BT), jnp.int32),
            pltpu.SemaphoreType.DMA((tiles,)),
            pltpu.SemaphoreType.DMA,
            pltpu.SemaphoreType.DMA,
            pltpu.SemaphoreType.DMA((15,)),
            pltpu.SemaphoreType.DMA,
            pltpu.SemaphoreType.DMA((tiles, 4)),
            pltpu.SemaphoreType.DMA((tiles, 11)),
            pltpu.SemaphoreType.DMA((half,)),
            pltpu.SemaphoreType.DMA((half,)),
        ],
        compiler_params=pltpu.CompilerParams(
            collective_id=0, has_side_effects=True, vmem_limit_bytes=48 * 2**20),
        name="correct",
    )(proj, dh, ids)


def solution(mesh):
    placed = (P("atom", None, "row"), P("atom", "row"), P("atom", None, None, None))
    return jax.shard_map(
        on_device, mesh=mesh, in_specs=placed, out_specs=P("row", ("col", "atom")), check_vma=False
    )
```

```python
import functools

import jax
import jax.numpy as jnp
from jax import lax
from jax.experimental import pallas as pl
from jax.experimental.pallas import tpu as pltpu
from jax.sharding import PartitionSpec as P

MESH = pl.DeviceIdType.MESH
BT = 128
PAD = 16


def kernel(proj, dht, nbh, out, nbt, pbuf, colb, dhv, tab, blocks, pt, sel, q, acc, xsend, xrecv,
           colx, col_s, fnd, fnd_s, lsem, dsem, isem, nsend, nrecv, rsem, ssem, xssem, xrsem):
    slots, ap, _ = proj.shape
    npj, _, atb, nats = dht.shape
    tiles = pbuf.shape[0]
    half = tiles // 2
    part = slots // 6
    row, c, a = lax.axis_index("row"), lax.axis_index("col"), lax.axis_index("atom")
    x, h, k = row // 4, (row // 2) % 2, row % 2
    xs, hs, ks = c // 4, (c // 2) % 2, c % 2
    is_root = row == c
    root_chip = (row // 2) == (c // 2)
    is_twin = root_chip & (row != c)
    e = (x - xs) % 4

    def dev(x_, h_, k_):
        return (x_ * 4 + h_ * 2 + k_, c, a)

    def tile_of(t):
        return (t + half * (1 - a)) % tiles

    bar = pltpu.get_barrier_semaphore()
    for i in range(1, 16):
        pl.semaphore_signal(bar, inc=1, device_id=((row + i) % 16, c, a), device_id_type=MESH)
    pl.semaphore_signal(bar, inc=1, device_id=(row, c, 1 - a), device_id_type=MESH)

    loads = [
        pltpu.make_async_copy(proj.at[:, :, pl.ds(i * BT, BT)], pbuf.at[i], lsem.at[i])
        for i in range(tiles)
    ]
    for cp in loads:
        cp.start()
    dcopy = pltpu.make_async_copy(dht, dhv, dsem)
    dcopy.start()
    ncopy = pltpu.make_async_copy(nbh, nbt, isem)
    ncopy.start()

    def piece(buf, i, p):
        return buf.at[i, pl.ds(part * p, part)]

    def send(src, t, p, slot, target):
        return pltpu.make_async_remote_copy(
            src_ref=src, dst_ref=piece(colb, t, p), send_sem=ssem.at[t, slot],
            recv_sem=rsem.at[t, p], device_id=target, device_id_type=MESH)

    def root_ids(i):
        return pltpu.make_async_remote_copy(
            src_ref=nbt, dst_ref=colx, send_sem=nsend.at[i - 1],
            recv_sem=nrecv, device_id=((row + i) % 16, c, a), device_id_type=MESH)

    def spread_out(src, i, t):
        return [send(piece(src, i, 2 * g + b), t, 2 * g + b, 2 * g + b,
                     dev((xs + 1 + g) % 4, hs, t % 2))
                for b in range(2) for g in (1, 0, 2)]

    def to_twin(t):
        return [send(piece(pbuf, tile_of(t), p), t, p, 6 + p, dev(xs, hs, 1 - ks))
                for p in range(6)]

    @pl.when(is_root)
    def _():
        for cp in loads:
            cp.wait()
        ncopy.wait()
        pl.semaphore_wait(bar, 16)
        for cp in spread_out(pbuf, tile_of(0), 0):
            cp.start()

        def odd(i, carry):
            for cp in to_twin(2 * i + 1):
                cp.start()
            return carry

        lax.fori_loop(0, half, odd, 0)
        for i in range(1, 16):
            root_ids(i).start()
        pltpu.make_async_copy(nbt, colx, nrecv).start()

        def even(i, carry):
            for cp in spread_out(pbuf, tile_of(2 * i), 2 * i):
                cp.start()
            return carry

        lax.fori_loop(1, half, even, 0)

        def rest(t, carry):
            @pl.when(t % 2 == 0)
            def _():
                for cp in to_twin(t):
                    cp.start()

            for p in range(6):
                pltpu.make_async_copy(
                    piece(pbuf, tile_of(t), p), piece(colb, t, p), rsem.at[t, p]).start()
            return carry

        lax.fori_loop(0, tiles, rest, 0)

    def arrived(t, p):
        pltpu.make_async_copy(piece(colb, t, p), piece(colb, t, p), rsem.at[t, p]).wait()

    def relay(t):
        return (k == t % 2) & jnp.logical_not(root_chip)

    def relay_first(t, b):
        p = 2 * jnp.maximum(e - 1, 0) + b
        mine = piece(colb, t, p)
        cross = send(mine, t, p, 6 + b, dev(x, 1 - h, k))
        along = [(send(mine, t, p, 8 + 3 * b + n, dev((x + d) % 4, h, k)),
                  ((e + d) % 4 != 0) | (h != hs))
                 for n, d in enumerate((2, 1, 3))]
        twin = send(mine, t, p, p, dev(x, h, 1 - k))
        return p, cross, along, twin

    def relay_rest(t):
        return [(p, (e == 0) | (e != p // 2 + 1),
                 send(piece(colb, t, p), t, p, p, dev(x, h, 1 - k))) for p in range(6)]

    def forward_first(t):
        @pl.when(relay(t) & (e > 0))
        def _():
            for b in range(2):
                p, cross, along, twin = relay_first(t, b)
                arrived(t, p)

                @pl.when(h == hs)
                def _():
                    cross.start()

                for cp, needed in along:
                    @pl.when(needed)
                    def _():
                        cp.start()

                twin.start()

    def forward_rest(t):
        @pl.when(relay(t))
        def _():
            for p, other, cp in relay_rest(t):
                @pl.when(other)
                def _():
                    arrived(t, p)
                    cp.start()

        @pl.when(jnp.logical_not(relay(t) | (is_twin & (t % 2 == 1))))
        def _():
            for p in range(6):
                arrived(t, p)

    ridx = lax.broadcasted_iota(jnp.int32, (npj * atb, BT), 0)
    cidx = lax.broadcasted_iota(jnp.int32, (npj * atb, BT), 1)
    order = (ridx & 7) * npj + (ridx >> 3) == cidx
    order = order.astype(jnp.float32).astype(jnp.bfloat16)
    turn = (((0,), (0,)), ((), ()))
    dcopy.wait()
    tab[:, npj:, :] = jnp.zeros((nats, PAD - npj, BT), jnp.float32)
    for i in range(npj):
        v = dhv[i].reshape(npj * atb, nats)
        hi = v.astype(jnp.bfloat16)
        lo = (v - hi.astype(jnp.float32)).astype(jnp.bfloat16)
        rows_i = lax.dot_general(hi, order, turn, preferred_element_type=jnp.float32)
        rows_i += lax.dot_general(lo, order, turn, preferred_element_type=jnp.float32)
        tab[:, i, :] = rows_i
    ridx = lax.broadcasted_iota(jnp.int32, (BT, BT), 0)
    cidx = lax.broadcasted_iota(jnp.int32, (BT, BT), 1)
    inside = cidx - (ridx >> 4) * npj
    inside = (inside >= 0) & (inside < npj)
    blocks[...] = inside.astype(jnp.float32).astype(jnp.bfloat16)

    @pl.when(jnp.logical_not(is_root))
    def _():
        for cp in loads:
            cp.wait()
        ncopy.wait()
        pl.semaphore_wait(bar, 16)

    @pl.when(is_twin)
    def _():
        def step(i, carry):
            t = 2 * i + 1
            for p in range(6):
                arrived(t, p)
            for cp in spread_out(colb, t, t):
                cp.start()
            return carry

        lax.fori_loop(0, half, step, 0)

    pidx = lax.broadcasted_iota(jnp.int32, (ap, BT), 0)
    sidx = lax.broadcasted_iota(jnp.int32, (ap, BT), 1)
    spread = ((sidx >> 4) * npj + (sidx & 15) == pidx) & ((sidx & 15) < npj)
    spread = spread.astype(jnp.float32).astype(jnp.bfloat16)

    def flip(u, carry):
        for l in range(slots):
            pt[u, l] = lax.dot_general(
                pbuf[u, l], spread, turn, preferred_element_type=jnp.float32).astype(jnp.bfloat16)
        pt[u, slots] = jnp.zeros((BT, BT), jnp.bfloat16)
        return carry

    lax.fori_loop(0, tiles, flip, 0)

    for t in range(4):
        forward_first(t)

    pltpu.make_async_copy(nbt, colx, nrecv).wait()
    ccopy = pltpu.make_async_copy(colx, col_s, isem)
    ccopy.start()
    ccopy.wait()
    rows_l = nbt[...]
    lidx = lax.broadcasted_iota(jnp.int32, (tiles, slots), 1)
    fidx = lax.broadcasted_iota(jnp.int32, (tiles, BT), 1)
    found = jnp.full((tiles, BT), slots, jnp.int32)
    for t in range(tiles):
        for m in range(slots):
            cs = col_s[t, m]
            hit = jnp.where((rows_l == cs) & (cs >= 0), lidx, slots)
            hit = jnp.min(hit, axis=1, keepdims=True)
            found = jnp.where(fidx == t * slots + m, hit, found)
    fnd[...] = found
    fcopy = pltpu.make_async_copy(fnd, fnd_s, isem)
    fcopy.start()
    fcopy.wait()

    def exchange(t):
        return pltpu.make_async_remote_copy(
            src_ref=xsend.at[t], dst_ref=xrecv.at[t], send_sem=xssem.at[t], recv_sem=xrsem.at[t],
            device_id=(row, c, 1 - a), device_id_type=MESH)

    def step(t, carry):
        forward_rest(t)

        @pl.when(t == 0)
        def _():
            forward_first(4)

        tile = tile_of(t)
        mask = blocks[...]
        for m in range(slots):
            v = tab[jnp.clip(col_s[tile, m] - a * nats, 0, nats - 1)]
            hi = v.astype(jnp.bfloat16)
            lo = (v - hi.astype(jnp.float32)).astype(jnp.bfloat16)
            hi = jnp.concatenate([hi] * atb, axis=0) * mask
            lo = jnp.concatenate([lo] * atb, axis=0) * mask
            piece = colb[t, m]
            prod = jnp.dot(hi[:, :ap], piece, preferred_element_type=jnp.float32)
            prod += jnp.dot(lo[:, :ap], piece, preferred_element_type=jnp.float32)
            q[m * BT:(m + 1) * BT, :] = prod.astype(jnp.bfloat16)
        for u in range(tiles):
            for m in range(slots):
                l = fnd_s[u, tile * slots + m]
                sel[u * BT:(u + 1) * BT, m * BT:(m + 1) * BT] = pt[u, l]
        block = jnp.dot(sel[...], q[...], preferred_element_type=jnp.float32)

        @pl.when(t < half)
        def _():
            xsend[t] = block.astype(jnp.bfloat16)
            exchange(t).start()

        @pl.when(t >= half)
        def _():
            acc[t - half] = block

        @pl.when(t == 0)
        def _():
            forward_first(5)

        return carry

    lax.fori_loop(0, tiles, step, 0)

    for j in range(half):
        exchange(j).wait_recv()
        out[:, j * BT:(j + 1) * BT] = acc[j] + xrecv[j].astype(jnp.float32)

    for j in range(half):
        exchange(j).wait_send()

    @pl.when(is_root)
    def _():
        for i in range(1, 16):
            root_ids(i).wait_send()

        def drain(t, carry):
            @pl.when(t % 2 == 0)
            def _():
                for cp in spread_out(pbuf, tile_of(t), t):
                    cp.wait_send()

            for cp in to_twin(t):
                cp.wait_send()
            return carry

        lax.fori_loop(0, tiles, drain, 0)

    @pl.when(is_twin)
    def _():
        def drain(i, carry):
            for cp in spread_out(colb, 2 * i + 1, 2 * i + 1):
                cp.wait_send()
            return carry

        lax.fori_loop(0, half, drain, 0)

    def drain(t, carry):
        @pl.when(relay(t))
        def _():
            @pl.when(e > 0)
            def _():
                for b in range(2):
                    p, cross, along, twin = relay_first(t, b)

                    @pl.when(h == hs)
                    def _():
                        cross.wait_send()

                    for cp, needed in along:
                        @pl.when(needed)
                        def _():
                            cp.wait_send()

                    twin.wait_send()

            for p, other, cp in relay_rest(t):
                @pl.when(other)
                def _():
                    cp.wait_send()

        return carry

    lax.fori_loop(0, tiles, drain, 0)


def on_device(proj, nbr, dh):
    slots, ap, rows = proj.shape
    tiles = nbr.shape[1]
    nats, atb, npj, _ = dh.shape
    half = tiles // 2
    dht = jnp.transpose(dh, (2, 3, 1, 0))
    bf, f32 = jnp.bfloat16, jnp.float32
    return pl.pallas_call(
        kernel,
        out_shape=jax.ShapeDtypeStruct((rows, half * BT), f32),
        in_specs=[pl.BlockSpec(memory_space=pltpu.HBM)] * 3,
        out_specs=pl.BlockSpec(memory_space=pltpu.VMEM),
        scratch_shapes=[
            pltpu.VMEM((tiles, slots), jnp.int32),
            pltpu.VMEM((tiles, slots, ap, BT), bf),
            pltpu.VMEM((tiles, slots, ap, BT), bf),
            pltpu.VMEM(dht.shape, f32),
            pltpu.VMEM((nats, PAD, BT), f32),
            pltpu.VMEM((BT, BT), bf),
            pltpu.VMEM((tiles, slots + 1, BT, BT), bf),
            pltpu.VMEM((rows, slots * BT), bf),
            pltpu.VMEM((slots * BT, BT), bf),
            pltpu.VMEM((half, rows, BT), f32),
            pltpu.VMEM((half, rows, BT), bf),
            pltpu.VMEM((half, rows, BT), bf),
            pltpu.VMEM((tiles, slots), jnp.int32),
            pltpu.SMEM((tiles, slots), jnp.int32),
            pltpu.VMEM((tiles, BT), jnp.int32),
            pltpu.SMEM((tiles, BT), jnp.int32),
            pltpu.SemaphoreType.DMA((tiles,)),
            pltpu.SemaphoreType.DMA,
            pltpu.SemaphoreType.DMA,
            pltpu.SemaphoreType.DMA((15,)),
            pltpu.SemaphoreType.DMA,
            pltpu.SemaphoreType.DMA((tiles, 6)),
            pltpu.SemaphoreType.DMA((tiles, 14)),
            pltpu.SemaphoreType.DMA((half,)),
            pltpu.SemaphoreType.DMA((half,)),
        ],
        compiler_params=pltpu.CompilerParams(
            collective_id=0, has_side_effects=True, vmem_limit_bytes=56 * 2**20),
        name="correct",
    )(proj, dht, nbr.T)


def solution(mesh):
    placed = (P("atom", None, "row"), P("atom", "row"), P("atom", None, None, None))
    return jax.shard_map(
        on_device, mesh=mesh, in_specs=placed, out_specs=P("row", ("col", "atom")), check_vma=False
    )
```

```python
import functools

import jax
import jax.numpy as jnp
from jax import lax
from jax.experimental import pallas as pl
from jax.experimental.pallas import tpu as pltpu
from jax.sharding import PartitionSpec as P

MESH = pl.DeviceIdType.MESH
BT = 128
PAD = 16


def kernel(proj, dht, nbh, own, theirs, nbt, pbuf, colb, dhv, tab, blocks, pt, q, acc, xsend,
           colx, col_s, fnd, fnd_s, lsem, dsem, isem, nsend, nrecv, rsem, ssem, xssem, xrsem, osem):
    slots, ap, _ = proj.shape
    npj, _, atb, nats = dht.shape
    tiles = pbuf.shape[0]
    half = tiles // 2
    share = slots // 6
    row, c, a = lax.axis_index("row"), lax.axis_index("col"), lax.axis_index("atom")
    x, h, k = row // 4, (row // 2) % 2, row % 2
    xs, hs, ks = c // 4, (c // 2) % 2, c % 2
    is_root = row == c
    root_chip = (row // 2) == (c // 2)
    is_twin = root_chip & (row != c)
    e = (x - xs) % 4

    def dev(x_, h_, k_):
        return (x_ * 4 + h_ * 2 + k_, c, a)

    def tile_of(t):
        return (t + half * (1 - a)) % tiles

    bar = pltpu.get_barrier_semaphore()
    for i in range(1, 16):
        pl.semaphore_signal(bar, inc=1, device_id=((row + i) % 16, c, a), device_id_type=MESH)
    pl.semaphore_signal(bar, inc=1, device_id=(row, c, 1 - a), device_id_type=MESH)

    loads = [
        pltpu.make_async_copy(proj.at[:, :, pl.ds(i * BT, BT)], pbuf.at[i], lsem.at[i])
        for i in range(tiles)
    ]
    for cp in loads:
        cp.start()
    dcopy = pltpu.make_async_copy(dht, dhv, dsem)
    dcopy.start()
    ncopy = pltpu.make_async_copy(nbh, nbt, isem)
    ncopy.start()

    def piece(buf, i, p):
        return buf.at[i, pl.ds(share * p, share)]

    def send(src, t, p, slot, target):
        return pltpu.make_async_remote_copy(
            src_ref=src, dst_ref=piece(colb, t, p), send_sem=ssem.at[t, slot],
            recv_sem=rsem.at[t, p], device_id=target, device_id_type=MESH)

    def root_ids(i):
        return pltpu.make_async_remote_copy(
            src_ref=nbt, dst_ref=colx, send_sem=nsend.at[i - 1],
            recv_sem=nrecv, device_id=((row + i) % 16, c, a), device_id_type=MESH)

    def spread_out(src, i, t, b):
        return [send(piece(src, i, 2 * g + b), t, 2 * g + b, 2 * g + b,
                     dev((xs + 1 + g) % 4, hs, b)) for g in ((1, 0, 2), (2, 1, 0))[b]]

    def to_twin(t, b):
        return [send(piece(pbuf, tile_of(t), 2 * g + b), t, 2 * g + b, 6 + 2 * g + b,
                     dev(xs, hs, 1 - ks)) for g in (1, 0, 2)]

    @pl.when(is_root)
    def _():
        for cp in loads:
            cp.wait()
        ncopy.wait()
        pl.semaphore_wait(bar, 16)

        def first(t, carry):
            for cp in to_twin(t, 1):
                cp.start()
            for cp in spread_out(pbuf, tile_of(t), t, 0):
                cp.start()
            return carry

        lax.fori_loop(0, 2, first, 0)
        for i in range(1, 16):
            root_ids(i).start()
        pltpu.make_async_copy(nbt, colx, nrecv).start()
        lax.fori_loop(2, tiles, first, 0)

        def rest(t, carry):
            for cp in to_twin(t, 0):
                cp.start()
            for p in range(6):
                pltpu.make_async_copy(
                    piece(pbuf, tile_of(t), p), piece(colb, t, p), rsem.at[t, p]).start()
            return carry

        lax.fori_loop(0, tiles, rest, 0)

    def arrived(t, p):
        pltpu.make_async_copy(piece(colb, t, p), piece(colb, t, p), rsem.at[t, p]).wait()

    relay = jnp.logical_not(root_chip)

    def relay_first(t):
        p = 2 * jnp.maximum(e - 1, 0) + k
        mine = piece(colb, t, p)
        cross = send(mine, t, p, 6, dev(x, 1 - h, k))
        hops = [n + 1 + k * (2 - 2 * n) for n in range(3)]
        along = [(send(mine, t, p, 7 + n, dev((x + d) % 4, h, k)),
                  ((e + d) % 4 != 0) | (h != hs)) for n, d in enumerate(hops)]
        twin = send(mine, t, p, p, dev(x, h, 1 - k))
        return p, cross, along, twin

    def relay_rest(t):
        return [(2 * g + k, e != g + 1,
                 send(piece(colb, t, 2 * g + k), t, 2 * g + k, 2 * g + k, dev(x, h, 1 - k)))
                for g in range(3)]

    def forward_first(t):
        @pl.when(relay & (e > 0))
        def _():
            p, cross, along, twin = relay_first(t)
            arrived(t, p)

            @pl.when(h == hs)
            def _():
                cross.start()

            for cp, needed in along:
                @pl.when(needed)
                def _():
                    cp.start()

            twin.start()

    def forward_rest(t):
        @pl.when(relay)
        def _():
            for p, other, cp in relay_rest(t):
                @pl.when(other)
                def _():
                    arrived(t, p)
                    cp.start()

    def complete(t):
        @pl.when(relay)
        def _():
            for g in range(3):
                arrived(t, 2 * g + 1 - k)

        @pl.when(root_chip)
        def _():
            for g in range(3):
                arrived(t, 2 * g)

        @pl.when(is_root)
        def _():
            for g in range(3):
                arrived(t, 2 * g + 1)

    ridx = lax.broadcasted_iota(jnp.int32, (npj * atb, BT), 0)
    cidx = lax.broadcasted_iota(jnp.int32, (npj * atb, BT), 1)
    order = (ridx & 7) * npj + (ridx >> 3) == cidx
    order = order.astype(jnp.float32).astype(jnp.bfloat16)
    turn = (((0,), (0,)), ((), ()))
    dcopy.wait()
    tab[:, npj:, :] = jnp.zeros((nats, PAD - npj, BT), jnp.float32)
    for i in range(npj):
        v = dhv[i].reshape(npj * atb, nats)
        hi = v.astype(jnp.bfloat16)
        lo = (v - hi.astype(jnp.float32)).astype(jnp.bfloat16)
        rows_i = lax.dot_general(hi, order, turn, preferred_element_type=jnp.float32)
        rows_i += lax.dot_general(lo, order, turn, preferred_element_type=jnp.float32)
        tab[:, i, :] = rows_i
    ridx = lax.broadcasted_iota(jnp.int32, (BT, BT), 0)
    cidx = lax.broadcasted_iota(jnp.int32, (BT, BT), 1)
    inside = cidx - (ridx >> 4) * npj
    inside = (inside >= 0) & (inside < npj)
    blocks[...] = inside.astype(jnp.float32).astype(jnp.bfloat16)

    @pl.when(jnp.logical_not(is_root))
    def _():
        for cp in loads:
            cp.wait()
        ncopy.wait()
        pl.semaphore_wait(bar, 16)

    @pl.when(is_twin)
    def _():
        def first(t, carry):
            for g in (1, 0, 2):
                arrived(t, 2 * g + 1)
            for cp in spread_out(colb, t, t, 1):
                cp.start()
            return carry

        lax.fori_loop(0, tiles, first, 0)

    pidx = lax.broadcasted_iota(jnp.int32, (ap, BT), 0)
    sidx = lax.broadcasted_iota(jnp.int32, (ap, BT), 1)
    spread = ((sidx >> 4) * npj + (sidx & 15) == pidx) & ((sidx & 15) < npj)
    spread = spread.astype(jnp.float32).astype(jnp.bfloat16)

    def flip(u, carry):
        for l in range(slots):
            pt[u, l] = lax.dot_general(
                pbuf[u, l], spread, turn, preferred_element_type=jnp.float32).astype(jnp.bfloat16)
        pt[u, slots] = jnp.zeros((BT, BT), jnp.bfloat16)
        return carry

    lax.fori_loop(0, tiles, flip, 0)

    for t in range(4):
        forward_first(t)

    pltpu.make_async_copy(nbt, colx, nrecv).wait()
    ccopy = pltpu.make_async_copy(colx, col_s, isem)
    ccopy.start()
    ccopy.wait()
    rows_l = nbt[...]
    lidx = lax.broadcasted_iota(jnp.int32, (tiles, slots), 1)
    fidx = lax.broadcasted_iota(jnp.int32, (tiles, BT), 1)
    found = jnp.full((tiles, BT), slots, jnp.int32)
    for t in range(tiles):
        for m in range(slots):
            cs = col_s[t, m]
            hit = jnp.where((rows_l == cs) & (cs >= 0), lidx, slots)
            hit = jnp.min(hit, axis=1, keepdims=True)
            found = jnp.where(fidx == t * slots + m, hit, found)
    fnd[...] = found
    fcopy = pltpu.make_async_copy(fnd, fnd_s, isem)
    fcopy.start()
    fcopy.wait()

    def part(ref, j, u):
        return ref.at[pl.ds(u * BT, BT), pl.ds(pl.multiple_of(j * BT, BT), BT)]

    def exchange(j, u):
        return pltpu.make_async_remote_copy(
            src_ref=xsend.at[j, u], dst_ref=part(theirs, j, u), send_sem=xssem.at[j, u],
            recv_sem=xrsem.at[j, u], device_id=(row, c, 1 - a), device_id_type=MESH)

    def keep(j, u):
        return pltpu.make_async_copy(acc.at[j, u], part(own, j, u), osem.at[j, u])

    forward_rest(0)
    forward_first(4)

    def step(t, carry):
        complete(t)

        @pl.when(t + 1 < tiles)
        def _():
            forward_rest(t + 1)

        @pl.when(t == 0)
        def _():
            forward_first(5)

        tile = tile_of(t)
        mask = blocks[...]
        for m in range(slots):
            v = tab[jnp.clip(col_s[tile, m] - a * nats, 0, nats - 1)]
            hi = v.astype(jnp.bfloat16)
            lo = (v - hi.astype(jnp.float32)).astype(jnp.bfloat16)
            hi = jnp.concatenate([hi] * atb, axis=0) * mask
            lo = jnp.concatenate([lo] * atb, axis=0) * mask
            piece = colb[t, m]
            prod = jnp.dot(hi[:, :ap], piece, preferred_element_type=jnp.float32)
            prod += jnp.dot(lo[:, :ap], piece, preferred_element_type=jnp.float32)
            q[m * BT:(m + 1) * BT, :] = prod.astype(jnp.bfloat16)
        for u in range(tiles):
            lhs = [pt[u, fnd_s[u, tile * slots + m]] for m in range(slots)]
            block = jnp.dot(jnp.concatenate(lhs, axis=1), q[...],
                            preferred_element_type=jnp.float32)

            @pl.when(t < half)
            def _():
                xsend[t, u] = block.astype(jnp.bfloat16)
                exchange(t, u).start()

            @pl.when(t >= half)
            def _():
                acc[t - half, u] = block
                keep(t - half, u).start()

        return carry

    lax.fori_loop(0, tiles, step, 0)

    def finish(j, carry):
        for u in range(tiles):
            keep(j, u).wait()
            exchange(j, u).wait_send()
            exchange(j, u).wait_recv()
        return carry

    lax.fori_loop(0, half, finish, 0)

    @pl.when(is_root)
    def _():
        for i in range(1, 16):
            root_ids(i).wait_send()

        def drain(t, carry):
            for b in range(2):
                for cp in to_twin(t, b):
                    cp.wait_send()
            for cp in spread_out(pbuf, tile_of(t), t, 0):
                cp.wait_send()
            return carry

        lax.fori_loop(0, tiles, drain, 0)

    @pl.when(is_twin)
    def _():
        def drain(t, carry):
            for cp in spread_out(colb, t, t, 1):
                cp.wait_send()
            return carry

        lax.fori_loop(0, tiles, drain, 0)

    @pl.when(relay)
    def _():
        def drain(t, carry):
            @pl.when(e > 0)
            def _():
                p, cross, along, twin = relay_first(t)

                @pl.when(h == hs)
                def _():
                    cross.wait_send()

                for cp, needed in along:
                    @pl.when(needed)
                    def _():
                        cp.wait_send()

                twin.wait_send()

            for p, other, cp in relay_rest(t):
                @pl.when(other)
                def _():
                    cp.wait_send()

            return carry

        lax.fori_loop(0, tiles, drain, 0)


def on_device(proj, nbr, dh):
    slots, ap, rows = proj.shape
    tiles = nbr.shape[1]
    nats, atb, npj, _ = dh.shape
    half = tiles // 2
    dht = jnp.transpose(dh, (2, 3, 1, 0))
    bf, f32 = jnp.bfloat16, jnp.float32
    own, theirs = pl.pallas_call(
        kernel,
        out_shape=[jax.ShapeDtypeStruct((rows, half * BT), f32),
                   jax.ShapeDtypeStruct((rows, half * BT), bf)],
        in_specs=[pl.BlockSpec(memory_space=pltpu.HBM)] * 3,
        out_specs=[pl.BlockSpec(memory_space=pl.ANY)] * 2,
        scratch_shapes=[
            pltpu.VMEM((tiles, slots), jnp.int32),
            pltpu.VMEM((tiles, slots, ap, BT), bf),
            pltpu.VMEM((tiles, slots, ap, BT), bf),
            pltpu.VMEM(dht.shape, f32),
            pltpu.VMEM((nats, PAD, BT), f32),
            pltpu.VMEM((BT, BT), bf),
            pltpu.VMEM((tiles, slots + 1, BT, BT), bf),
            pltpu.VMEM((slots * BT, BT), bf),
            pltpu.VMEM((half, tiles, BT, BT), f32),
            pltpu.VMEM((half, tiles, BT, BT), bf),
            pltpu.VMEM((tiles, slots), jnp.int32),
            pltpu.SMEM((tiles, slots), jnp.int32),
            pltpu.VMEM((tiles, BT), jnp.int32),
            pltpu.SMEM((tiles, BT), jnp.int32),
            pltpu.SemaphoreType.DMA((tiles,)),
            pltpu.SemaphoreType.DMA,
            pltpu.SemaphoreType.DMA,
            pltpu.SemaphoreType.DMA((15,)),
            pltpu.SemaphoreType.DMA,
            pltpu.SemaphoreType.DMA((tiles, 6)),
            pltpu.SemaphoreType.DMA((tiles, 12)),
            pltpu.SemaphoreType.DMA((half, tiles)),
            pltpu.SemaphoreType.DMA((half, tiles)),
            pltpu.SemaphoreType.DMA((half, tiles)),
        ],
        compiler_params=pltpu.CompilerParams(
            collective_id=0, has_side_effects=True, vmem_limit_bytes=56 * 2**20),
        name="correct",
    )(proj, dht, nbr.T)
    return own + theirs.astype(f32)


def solution(mesh):
    placed = (P("atom", None, "row"), P("atom", "row"), P("atom", None, None, None))
    return jax.shard_map(
        on_device, mesh=mesh, in_specs=placed, out_specs=P("row", ("col", "atom")), check_vma=False
    )
```

```python
import functools

import jax
import jax.numpy as jnp
from jax import lax
from jax.experimental import pallas as pl
from jax.experimental.pallas import tpu as pltpu
from jax.sharding import PartitionSpec as P

MESH = pl.DeviceIdType.MESH
BT = 128
PAD = 16


def kernel(proj, dht, nbh, own, theirs, nbt, pbuf, colb, dhv, tab, blocks, pt, q, acc, xsend,
           colx, col_s, fnd, fnd_s, lsem, dsem, isem, nsend, nrecv, rsem, ssem, xssem, xrsem, osem):
    slots, ap, _ = proj.shape
    npj, _, atb, nats = dht.shape
    tiles = pbuf.shape[0]
    half = tiles // 2
    share = slots // 6
    row, c, a = lax.axis_index("row"), lax.axis_index("col"), lax.axis_index("atom")
    x, h, k = row // 4, (row // 2) % 2, row % 2
    xs, hs, ks = c // 4, (c // 2) % 2, c % 2
    is_root = row == c
    root_chip = (row // 2) == (c // 2)
    is_twin = root_chip & (row != c)
    e = (x - xs) % 4

    def dev(x_, h_, k_):
        return (x_ * 4 + h_ * 2 + k_, c, a)

    def tile_of(t):
        return (t + half * (1 - a)) % tiles

    bar = pltpu.get_barrier_semaphore()
    for i in range(1, 16):
        pl.semaphore_signal(bar, inc=1, device_id=((row + i) % 16, c, a), device_id_type=MESH)
    pl.semaphore_signal(bar, inc=1, device_id=(row, c, 1 - a), device_id_type=MESH)

    loads = [
        pltpu.make_async_copy(proj.at[:, :, pl.ds(i * BT, BT)], pbuf.at[i], lsem.at[i])
        for i in range(tiles)
    ]
    for cp in loads:
        cp.start()
    dcopy = pltpu.make_async_copy(dht, dhv, dsem)
    dcopy.start()
    ncopy = pltpu.make_async_copy(nbh, nbt, isem)
    ncopy.start()

    def piece(buf, i, p):
        return buf.at[i, pl.ds(share * p, share)]

    def send(src, t, p, slot, target):
        return pltpu.make_async_remote_copy(
            src_ref=src, dst_ref=piece(colb, t, p), send_sem=ssem.at[t, slot],
            recv_sem=rsem.at[t, p], device_id=target, device_id_type=MESH)

    def root_ids(i):
        return pltpu.make_async_remote_copy(
            src_ref=nbt, dst_ref=colx, send_sem=nsend.at[i - 1],
            recv_sem=nrecv, device_id=((row + i) % 16, c, a), device_id_type=MESH)

    def spread_out(src, i, t, b):
        return [send(piece(src, i, 2 * g + b), t, 2 * g + b, 2 * g + b,
                     dev((xs + 1 + g) % 4, hs, b)) for g in ((1, 0, 2), (2, 1, 0))[b]]

    def to_twin(t, b):
        return [send(piece(pbuf, tile_of(t), 2 * g + b), t, 2 * g + b, 6 + 2 * g + b,
                     dev(xs, hs, 1 - ks)) for g in (1, 0, 2)]

    @pl.when(is_root)
    def _():
        for cp in loads:
            cp.wait()
        ncopy.wait()
        pl.semaphore_wait(bar, 16)

        for cp in to_twin(0, 1):
            cp.start()

        def first(t, carry):
            @pl.when(t + 1 < tiles)
            def _():
                for cp in to_twin(t + 1, 1):
                    cp.start()

            for cp in spread_out(pbuf, tile_of(t), t, 0):
                cp.start()
            return carry

        lax.fori_loop(0, 2, first, 0)
        for i in range(1, 16):
            root_ids(i).start()
        pltpu.make_async_copy(nbt, colx, nrecv).start()
        lax.fori_loop(2, tiles, first, 0)

        def rest(t, carry):
            for cp in to_twin(t, 0):
                cp.start()
            for p in range(6):
                pltpu.make_async_copy(
                    piece(pbuf, tile_of(t), p), piece(colb, t, p), rsem.at[t, p]).start()
            return carry

        lax.fori_loop(0, tiles, rest, 0)

    def arrived(t, p):
        pltpu.make_async_copy(piece(colb, t, p), piece(colb, t, p), rsem.at[t, p]).wait()

    relay = jnp.logical_not(root_chip)

    def relay_first(t):
        p = 2 * jnp.maximum(e - 1, 0) + k
        mine = piece(colb, t, p)
        cross = send(mine, t, p, 6, dev(x, 1 - h, k))
        hops = [n + 1 + k * (2 - 2 * n) for n in range(3)]
        along = [(send(mine, t, p, 7 + n, dev((x + d) % 4, h, k)),
                  ((e + d) % 4 != 0) | (h != hs)) for n, d in enumerate(hops)]
        twin = send(mine, t, p, p, dev(x, h, 1 - k))
        return p, cross, along, twin

    def relay_rest(t):
        return [(2 * g + k, e != g + 1,
                 send(piece(colb, t, 2 * g + k), t, 2 * g + k, 2 * g + k, dev(x, h, 1 - k)))
                for g in range(3)]

    def forward_first(t):
        @pl.when(relay & (e > 0))
        def _():
            p, cross, along, twin = relay_first(t)
            arrived(t, p)

            @pl.when(h == hs)
            def _():
                cross.start()

            for cp, needed in along:
                @pl.when(needed)
                def _():
                    cp.start()

            twin.start()

    def forward_rest(t):
        @pl.when(relay)
        def _():
            for p, other, cp in relay_rest(t):
                @pl.when(other)
                def _():
                    arrived(t, p)
                    cp.start()

    def complete(t):
        @pl.when(relay)
        def _():
            for g in range(3):
                arrived(t, 2 * g + 1 - k)

        @pl.when(root_chip)
        def _():
            for g in range(3):
                arrived(t, 2 * g)

        @pl.when(is_root)
        def _():
            for g in range(3):
                arrived(t, 2 * g + 1)

    ridx = lax.broadcasted_iota(jnp.int32, (npj * atb, BT), 0)
    cidx = lax.broadcasted_iota(jnp.int32, (npj * atb, BT), 1)
    order = (ridx & 7) * npj + (ridx >> 3) == cidx
    order = order.astype(jnp.float32).astype(jnp.bfloat16)
    turn = (((0,), (0,)), ((), ()))
    dcopy.wait()
    tab[:, npj:, :] = jnp.zeros((nats, PAD - npj, BT), jnp.float32)
    for i in range(npj):
        v = dhv[i].reshape(npj * atb, nats)
        hi = v.astype(jnp.bfloat16)
        lo = (v - hi.astype(jnp.float32)).astype(jnp.bfloat16)
        rows_i = lax.dot_general(hi, order, turn, preferred_element_type=jnp.float32)
        rows_i += lax.dot_general(lo, order, turn, preferred_element_type=jnp.float32)
        tab[:, i, :] = rows_i
    ridx = lax.broadcasted_iota(jnp.int32, (BT, BT), 0)
    cidx = lax.broadcasted_iota(jnp.int32, (BT, BT), 1)
    inside = cidx - (ridx >> 4) * npj
    inside = (inside >= 0) & (inside < npj)
    blocks[...] = inside.astype(jnp.float32).astype(jnp.bfloat16)

    @pl.when(jnp.logical_not(is_root))
    def _():
        for cp in loads:
            cp.wait()
        ncopy.wait()
        pl.semaphore_wait(bar, 16)

    @pl.when(is_twin)
    def _():
        def first(t, carry):
            for g in (1, 0, 2):
                arrived(t, 2 * g + 1)
            for cp in spread_out(colb, t, t, 1):
                cp.start()
            return carry

        lax.fori_loop(0, tiles, first, 0)

    pidx = lax.broadcasted_iota(jnp.int32, (ap, BT), 0)
    sidx = lax.broadcasted_iota(jnp.int32, (ap, BT), 1)
    spread = ((sidx >> 4) * npj + (sidx & 15) == pidx) & ((sidx & 15) < npj)
    spread = spread.astype(jnp.float32).astype(jnp.bfloat16)

    def flip(u, carry):
        for l in range(slots):
            pt[u, l] = lax.dot_general(
                pbuf[u, l], spread, turn, preferred_element_type=jnp.float32).astype(jnp.bfloat16)
        pt[u, slots] = jnp.zeros((BT, BT), jnp.bfloat16)
        return carry

    lax.fori_loop(0, tiles, flip, 0)

    for t in range(3):
        forward_first(t)

    pltpu.make_async_copy(nbt, colx, nrecv).wait()
    ccopy = pltpu.make_async_copy(colx, col_s, isem)
    ccopy.start()
    ccopy.wait()
    rows_l = nbt[...]
    lidx = lax.broadcasted_iota(jnp.int32, (tiles, slots), 1)
    fidx = lax.broadcasted_iota(jnp.int32, (tiles, BT), 1)
    found = jnp.full((tiles, BT), slots, jnp.int32)
    for t in range(tiles):
        for m in range(slots):
            cs = col_s[t, m]
            hit = jnp.where((rows_l == cs) & (cs >= 0), lidx, slots)
            hit = jnp.min(hit, axis=1, keepdims=True)
            found = jnp.where(fidx == t * slots + m, hit, found)
    fnd[...] = found
    fcopy = pltpu.make_async_copy(fnd, fnd_s, isem)
    fcopy.start()
    fcopy.wait()

    def part(ref, j, i):
        return ref.at[pl.ds(2 * i, 2), :, pl.ds(pl.multiple_of(j * BT, BT), BT)]

    def exchange(j, i):
        return pltpu.make_async_remote_copy(
            src_ref=xsend.at[j, pl.ds(2 * i, 2)], dst_ref=part(theirs, j, i), send_sem=xssem.at[j, i],
            recv_sem=xrsem.at[j, i], device_id=(row, c, 1 - a), device_id_type=MESH)

    def keep(j, i):
        return pltpu.make_async_copy(acc.at[j, pl.ds(2 * i, 2)], part(own, j, i), osem.at[j, i])

    forward_rest(0)

    def step(t, carry):
        complete(t)
        tile = tile_of(t)
        mask = blocks[...]
        for m in range(slots):
            v = tab[jnp.clip(col_s[tile, m] - a * nats, 0, nats - 1)]
            hi = v.astype(jnp.bfloat16)
            lo = (v - hi.astype(jnp.float32)).astype(jnp.bfloat16)
            hi = jnp.concatenate([hi] * atb, axis=0) * mask
            lo = jnp.concatenate([lo] * atb, axis=0) * mask
            piece = colb[t, m]
            prod = jnp.dot(hi[:, :ap], piece, preferred_element_type=jnp.float32)
            prod += jnp.dot(lo[:, :ap], piece, preferred_element_type=jnp.float32)
            q[m * BT:(m + 1) * BT, :] = prod.astype(jnp.bfloat16)
        def two(i, carry):
            blocks = []
            for n in range(2):
                u = 2 * i + n
                lhs = [pt[u, fnd_s[u, tile * slots + m]] for m in range(slots)]
                blocks.append(jnp.dot(jnp.concatenate(lhs, axis=1), q[...],
                                      preferred_element_type=jnp.float32))

            @pl.when(t < half)
            def _():
                for n in range(2):
                    xsend[t, 2 * i + n] = blocks[n].astype(jnp.bfloat16)

            @pl.when(t >= half)
            def _():
                for n in range(2):
                    acc[t - half, 2 * i + n] = blocks[n]
                keep(t - half, i).start()

            return carry

        lax.fori_loop(0, half, two, 0)

        @pl.when(t == 0)
        def _():
            forward_first(3)
            forward_first(4)
            forward_rest(1)
            forward_first(5)

        @pl.when((t > 0) & (t + 1 < tiles))
        def _():
            forward_rest(t + 1)

        @pl.when(t < half)
        def _():
            for i in range(half):
                exchange(t, i).start()

        return carry

    lax.fori_loop(0, tiles, step, 0)

    def finish(j, carry):
        for i in range(half):
            keep(j, i).wait()
            exchange(j, i).wait_send()
            exchange(j, i).wait_recv()
        return carry

    lax.fori_loop(0, half, finish, 0)

    @pl.when(is_root)
    def _():
        for i in range(1, 16):
            root_ids(i).wait_send()

        def drain(t, carry):
            for b in range(2):
                for cp in to_twin(t, b):
                    cp.wait_send()
            for cp in spread_out(pbuf, tile_of(t), t, 0):
                cp.wait_send()
            return carry

        lax.fori_loop(0, tiles, drain, 0)

    @pl.when(is_twin)
    def _():
        def drain(t, carry):
            for cp in spread_out(colb, t, t, 1):
                cp.wait_send()
            return carry

        lax.fori_loop(0, tiles, drain, 0)

    @pl.when(relay)
    def _():
        def drain(t, carry):
            @pl.when(e > 0)
            def _():
                p, cross, along, twin = relay_first(t)

                @pl.when(h == hs)
                def _():
                    cross.wait_send()

                for cp, needed in along:
                    @pl.when(needed)
                    def _():
                        cp.wait_send()

                twin.wait_send()

            for p, other, cp in relay_rest(t):
                @pl.when(other)
                def _():
                    cp.wait_send()

            return carry

        lax.fori_loop(0, tiles, drain, 0)


def on_device(proj, nbr, dh):
    slots, ap, rows = proj.shape
    tiles = nbr.shape[1]
    nats, atb, npj, _ = dh.shape
    half = tiles // 2
    dht = jnp.transpose(dh, (2, 3, 1, 0))
    bf, f32 = jnp.bfloat16, jnp.float32
    own, theirs = pl.pallas_call(
        kernel,
        out_shape=[jax.ShapeDtypeStruct((tiles, BT, half * BT), f32),
                   jax.ShapeDtypeStruct((tiles, BT, half * BT), bf)],
        in_specs=[pl.BlockSpec(memory_space=pltpu.HBM)] * 3,
        out_specs=[pl.BlockSpec(memory_space=pl.ANY)] * 2,
        scratch_shapes=[
            pltpu.VMEM((tiles, slots), jnp.int32),
            pltpu.VMEM((tiles, slots, ap, BT), bf),
            pltpu.VMEM((tiles, slots, ap, BT), bf),
            pltpu.VMEM(dht.shape, f32),
            pltpu.VMEM((nats, PAD, BT), f32),
            pltpu.VMEM((BT, BT), bf),
            pltpu.VMEM((tiles, slots + 1, BT, BT), bf),
            pltpu.VMEM((slots * BT, BT), bf),
            pltpu.VMEM((half, tiles, BT, BT), f32),
            pltpu.VMEM((half, tiles, BT, BT), bf),
            pltpu.VMEM((tiles, slots), jnp.int32),
            pltpu.SMEM((tiles, slots), jnp.int32),
            pltpu.VMEM((tiles, BT), jnp.int32),
            pltpu.SMEM((tiles, BT), jnp.int32),
            pltpu.SemaphoreType.DMA((tiles,)),
            pltpu.SemaphoreType.DMA,
            pltpu.SemaphoreType.DMA,
            pltpu.SemaphoreType.DMA((15,)),
            pltpu.SemaphoreType.DMA,
            pltpu.SemaphoreType.DMA((tiles, 6)),
            pltpu.SemaphoreType.DMA((tiles, 12)),
            pltpu.SemaphoreType.DMA((half, tiles)),
            pltpu.SemaphoreType.DMA((half, tiles)),
            pltpu.SemaphoreType.DMA((half, tiles)),
        ],
        compiler_params=pltpu.CompilerParams(
            collective_id=0, has_side_effects=True, vmem_limit_bytes=56 * 2**20),
        name="correct",
    )(proj, dht, nbr.T)
    return (own + theirs.astype(f32)).reshape(rows, half * BT)


def solution(mesh):
    placed = (P("atom", None, "row"), P("atom", "row"), P("atom", None, None, None))
    return jax.shard_map(
        on_device, mesh=mesh, in_specs=placed, out_specs=P("row", ("col", "atom")), check_vma=False
    )
```

```python
import functools

import jax
import jax.numpy as jnp
from jax import lax
from jax.experimental import pallas as pl
from jax.experimental.pallas import tpu as pltpu
from jax.sharding import PartitionSpec as P

MESH = pl.DeviceIdType.MESH
BT = 128
PAD = 16


def kernel(proj, dht, nbh, own, theirs, nbt, pbuf, colb, dhv, tab, blocks, pt, q, acc, xsend,
           colx, col_s, fnd, fnd_s, lsem, dsem, isem, nsend, nrecv, rsem, ssem, xssem, xrsem, osem):
    slots, ap, _ = proj.shape
    npj, _, atb, nats = dht.shape
    tiles = pbuf.shape[0]
    half = tiles // 2
    share = slots // 6
    row, c, a = lax.axis_index("row"), lax.axis_index("col"), lax.axis_index("atom")
    x, h, k = row // 4, (row // 2) % 2, row % 2
    xs, hs, ks = c // 4, (c // 2) % 2, c % 2
    is_root = row == c
    root_chip = (row // 2) == (c // 2)
    is_twin = root_chip & (row != c)
    e = (x - xs) % 4

    def dev(x_, h_, k_):
        return (x_ * 4 + h_ * 2 + k_, c, a)

    def tile_of(t):
        return (t + half * (1 - a)) % tiles

    bar = pltpu.get_barrier_semaphore()
    for i in range(1, 16):
        pl.semaphore_signal(bar, inc=1, device_id=((row + i) % 16, c, a), device_id_type=MESH)
    pl.semaphore_signal(bar, inc=1, device_id=(row, c, 1 - a), device_id_type=MESH)

    loads = [
        pltpu.make_async_copy(proj.at[:, :, pl.ds(i * BT, BT)], pbuf.at[i], lsem.at[i])
        for i in range(tiles)
    ]
    for cp in loads:
        cp.start()
    dcopy = pltpu.make_async_copy(dht, dhv, dsem)
    dcopy.start()
    ncopy = pltpu.make_async_copy(nbh, nbt, isem)
    ncopy.start()

    def piece(buf, i, p):
        return buf.at[i, pl.ds(share * p, share)]

    def send(src, t, p, slot, target):
        return pltpu.make_async_remote_copy(
            src_ref=src, dst_ref=piece(colb, t, p), send_sem=ssem.at[t, slot],
            recv_sem=rsem.at[t, p], device_id=target, device_id_type=MESH)

    def root_ids(i):
        return pltpu.make_async_remote_copy(
            src_ref=nbt, dst_ref=colx, send_sem=nsend.at[i - 1],
            recv_sem=nrecv, device_id=((row + i) % 16, c, a), device_id_type=MESH)

    def spread_out(src, i, t, b):
        return [send(piece(src, i, 2 * g + b), t, 2 * g + b, 2 * g + b,
                     dev((xs + 1 + g) % 4, hs, b)) for g in ((1, 0, 2), (2, 1, 0))[b]]

    def to_twin(t, b):
        return [send(piece(pbuf, tile_of(t), 2 * g + b), t, 2 * g + b, 6 + 2 * g + b,
                     dev(xs, hs, 1 - ks)) for g in (1, 0, 2)]

    @pl.when(is_root)
    def _():
        for cp in loads:
            cp.wait()
        ncopy.wait()
        pl.semaphore_wait(bar, 16)

        for cp in to_twin(0, 1):
            cp.start()

        def first(t, carry):
            @pl.when(t + 1 < tiles)
            def _():
                for cp in to_twin(t + 1, 1):
                    cp.start()

            for cp in spread_out(pbuf, tile_of(t), t, 0):
                cp.start()
            return carry

        lax.fori_loop(0, 4, first, 0)
        for i in range(1, 16):
            root_ids(i).start()
        pltpu.make_async_copy(nbt, colx, nrecv).start()
        lax.fori_loop(4, tiles, first, 0)

        def rest(t, carry):
            for cp in to_twin(t, 0):
                cp.start()
            for p in range(6):
                pltpu.make_async_copy(
                    piece(pbuf, tile_of(t), p), piece(colb, t, p), rsem.at[t, p]).start()
            return carry

        lax.fori_loop(0, tiles, rest, 0)

    def arrived(t, p):
        pltpu.make_async_copy(piece(colb, t, p), piece(colb, t, p), rsem.at[t, p]).wait()

    relay = jnp.logical_not(root_chip)

    def relay_first(t):
        p = 2 * jnp.maximum(e - 1, 0) + k
        mine = piece(colb, t, p)
        cross = send(mine, t, p, 6, dev(x, 1 - h, k))
        hops = [n + 1 + k * (2 - 2 * n) for n in range(3)]
        along = [(send(mine, t, p, 7 + n, dev((x + d) % 4, h, k)),
                  ((e + d) % 4 != 0) | (h != hs)) for n, d in enumerate(hops)]
        twin = send(mine, t, p, p, dev(x, h, 1 - k))
        return p, cross, along, twin

    def relay_rest(t):
        return [(2 * g + k, e != g + 1,
                 send(piece(colb, t, 2 * g + k), t, 2 * g + k, 2 * g + k, dev(x, h, 1 - k)))
                for g in range(3)]

    def forward_first(t):
        @pl.when(relay & (e > 0))
        def _():
            p, cross, along, twin = relay_first(t)
            arrived(t, p)

            @pl.when(h == hs)
            def _():
                cross.start()

            for cp, needed in along:
                @pl.when(needed)
                def _():
                    cp.start()

            twin.start()

    def forward_rest(t):
        @pl.when(relay)
        def _():
            for p, other, cp in relay_rest(t):
                @pl.when(other)
                def _():
                    arrived(t, p)
                    cp.start()

    def complete(t):
        @pl.when(relay)
        def _():
            for g in range(3):
                arrived(t, 2 * g + 1 - k)

        @pl.when(root_chip)
        def _():
            for g in range(3):
                arrived(t, 2 * g)

        @pl.when(is_root)
        def _():
            for g in range(3):
                arrived(t, 2 * g + 1)

    ridx = lax.broadcasted_iota(jnp.int32, (npj * atb, BT), 0)
    cidx = lax.broadcasted_iota(jnp.int32, (npj * atb, BT), 1)
    order = (ridx & 7) * npj + (ridx >> 3) == cidx
    order = order.astype(jnp.float32).astype(jnp.bfloat16)
    turn = (((0,), (0,)), ((), ()))
    dcopy.wait()
    tab[:, npj:, :] = jnp.zeros((nats, PAD - npj, BT), jnp.float32)
    for i in range(npj):
        v = dhv[i].reshape(npj * atb, nats)
        hi = v.astype(jnp.bfloat16)
        lo = (v - hi.astype(jnp.float32)).astype(jnp.bfloat16)
        rows_i = lax.dot_general(hi, order, turn, preferred_element_type=jnp.float32)
        rows_i += lax.dot_general(lo, order, turn, preferred_element_type=jnp.float32)
        tab[:, i, :] = rows_i
    ridx = lax.broadcasted_iota(jnp.int32, (BT, BT), 0)
    cidx = lax.broadcasted_iota(jnp.int32, (BT, BT), 1)
    inside = cidx - (ridx >> 4) * npj
    inside = (inside >= 0) & (inside < npj)
    blocks[...] = inside.astype(jnp.float32).astype(jnp.bfloat16)

    @pl.when(jnp.logical_not(is_root))
    def _():
        for cp in loads:
            cp.wait()
        ncopy.wait()
        pl.semaphore_wait(bar, 16)

    @pl.when(is_twin)
    def _():
        def first(t, carry):
            for g in (1, 0, 2):
                arrived(t, 2 * g + 1)
            for cp in spread_out(colb, t, t, 1):
                cp.start()
            return carry

        lax.fori_loop(0, tiles, first, 0)

    pidx = lax.broadcasted_iota(jnp.int32, (ap, BT), 0)
    sidx = lax.broadcasted_iota(jnp.int32, (ap, BT), 1)
    spread = ((sidx >> 4) * npj + (sidx & 15) == pidx) & ((sidx & 15) < npj)
    spread = spread.astype(jnp.float32).astype(jnp.bfloat16)

    def flip(u, carry):
        for l in range(slots):
            pt[u, l] = lax.dot_general(
                pbuf[u, l], spread, turn, preferred_element_type=jnp.float32).astype(jnp.bfloat16)
        pt[u, slots] = jnp.zeros((BT, BT), jnp.bfloat16)
        return carry

    lax.fori_loop(0, tiles, flip, 0)

    for t in range(3):
        forward_first(t)

    pltpu.make_async_copy(nbt, colx, nrecv).wait()
    ccopy = pltpu.make_async_copy(colx, col_s, isem)
    ccopy.start()
    ccopy.wait()
    rows_l = nbt[...]
    lidx = lax.broadcasted_iota(jnp.int32, (tiles, slots), 1)
    fidx = lax.broadcasted_iota(jnp.int32, (tiles, BT), 1)
    found = jnp.full((tiles, BT), slots, jnp.int32)
    for t in range(tiles):
        for m in range(slots):
            cs = col_s[t, m]
            hit = jnp.where((rows_l == cs) & (cs >= 0), lidx, slots)
            hit = jnp.min(hit, axis=1, keepdims=True)
            found = jnp.where(fidx == t * slots + m, hit, found)
    fnd[...] = found
    fcopy = pltpu.make_async_copy(fnd, fnd_s, isem)
    fcopy.start()
    fcopy.wait()

    def part(ref, j, i):
        return ref.at[pl.ds(2 * i, 2), :, pl.ds(pl.multiple_of(j * BT, BT), BT)]

    def exchange(j, i):
        return pltpu.make_async_remote_copy(
            src_ref=xsend.at[j, pl.ds(2 * i, 2)], dst_ref=part(theirs, j, i), send_sem=xssem.at[j, i],
            recv_sem=xrsem.at[j, i], device_id=(row, c, 1 - a), device_id_type=MESH)

    def keep(j, i):
        return pltpu.make_async_copy(acc.at[j, pl.ds(2 * i, 2)], part(own, j, i), osem.at[j, i])

    forward_rest(0)

    def step(t, carry):
        complete(t)
        tile = tile_of(t)
        mask = blocks[...]
        for m in range(slots):
            v = tab[jnp.clip(col_s[tile, m] - a * nats, 0, nats - 1)]
            hi = v.astype(jnp.bfloat16)
            lo = (v - hi.astype(jnp.float32)).astype(jnp.bfloat16)
            hi = jnp.concatenate([hi] * atb, axis=0) * mask
            lo = jnp.concatenate([lo] * atb, axis=0) * mask
            piece = colb[t, m]
            prod = jnp.dot(hi[:, :ap], piece, preferred_element_type=jnp.float32)
            prod += jnp.dot(lo[:, :ap], piece, preferred_element_type=jnp.float32)
            q[m * BT:(m + 1) * BT, :] = prod.astype(jnp.bfloat16)
        def two(i, carry):
            blocks = []
            for n in range(2):
                u = 2 * i + n
                lhs = [pt[u, fnd_s[u, tile * slots + m]] for m in range(slots)]
                blocks.append(jnp.dot(jnp.concatenate(lhs, axis=1), q[...],
                                      preferred_element_type=jnp.float32))

            @pl.when(t < half)
            def _():
                for n in range(2):
                    xsend[t, 2 * i + n] = blocks[n].astype(jnp.bfloat16)

            @pl.when(t >= half)
            def _():
                for n in range(2):
                    acc[t - half, 2 * i + n] = blocks[n]
                keep(t - half, i).start()

            return carry

        lax.fori_loop(0, half, two, 0)

        @pl.when(t == 0)
        def _():
            forward_first(3)
            forward_first(4)
            forward_rest(1)
            forward_first(5)

        @pl.when((t > 0) & (t + 1 < tiles))
        def _():
            forward_rest(t + 1)

        @pl.when(t < half)
        def _():
            for i in range(half):
                exchange(t, i).start()

        return carry

    lax.fori_loop(0, tiles, step, 0)

    def finish(j, carry):
        for i in range(half):
            keep(j, i).wait()
            exchange(j, i).wait_send()
            exchange(j, i).wait_recv()
        return carry

    lax.fori_loop(0, half, finish, 0)

    @pl.when(is_root)
    def _():
        for i in range(1, 16):
            root_ids(i).wait_send()

        def drain(t, carry):
            for b in range(2):
                for cp in to_twin(t, b):
                    cp.wait_send()
            for cp in spread_out(pbuf, tile_of(t), t, 0):
                cp.wait_send()
            return carry

        lax.fori_loop(0, tiles, drain, 0)

    @pl.when(is_twin)
    def _():
        def drain(t, carry):
            for cp in spread_out(colb, t, t, 1):
                cp.wait_send()
            return carry

        lax.fori_loop(0, tiles, drain, 0)

    @pl.when(relay)
    def _():
        def drain(t, carry):
            @pl.when(e > 0)
            def _():
                p, cross, along, twin = relay_first(t)

                @pl.when(h == hs)
                def _():
                    cross.wait_send()

                for cp, needed in along:
                    @pl.when(needed)
                    def _():
                        cp.wait_send()

                twin.wait_send()

            for p, other, cp in relay_rest(t):
                @pl.when(other)
                def _():
                    cp.wait_send()

            return carry

        lax.fori_loop(0, tiles, drain, 0)


def on_device(proj, nbr, dh):
    slots, ap, rows = proj.shape
    tiles = nbr.shape[1]
    nats, atb, npj, _ = dh.shape
    half = tiles // 2
    dht = jnp.transpose(dh, (2, 3, 1, 0))
    bf, f32 = jnp.bfloat16, jnp.float32
    own, theirs = pl.pallas_call(
        kernel,
        out_shape=[jax.ShapeDtypeStruct((tiles, BT, half * BT), f32),
                   jax.ShapeDtypeStruct((tiles, BT, half * BT), bf)],
        in_specs=[pl.BlockSpec(memory_space=pltpu.HBM)] * 3,
        out_specs=[pl.BlockSpec(memory_space=pl.ANY)] * 2,
        scratch_shapes=[
            pltpu.VMEM((tiles, slots), jnp.int32),
            pltpu.VMEM((tiles, slots, ap, BT), bf),
            pltpu.VMEM((tiles, slots, ap, BT), bf),
            pltpu.VMEM(dht.shape, f32),
            pltpu.VMEM((nats, PAD, BT), f32),
            pltpu.VMEM((BT, BT), bf),
            pltpu.VMEM((tiles, slots + 1, BT, BT), bf),
            pltpu.VMEM((slots * BT, BT), bf),
            pltpu.VMEM((half, tiles, BT, BT), f32),
            pltpu.VMEM((half, tiles, BT, BT), bf),
            pltpu.VMEM((tiles, slots), jnp.int32),
            pltpu.SMEM((tiles, slots), jnp.int32),
            pltpu.VMEM((tiles, BT), jnp.int32),
            pltpu.SMEM((tiles, BT), jnp.int32),
            pltpu.SemaphoreType.DMA((tiles,)),
            pltpu.SemaphoreType.DMA,
            pltpu.SemaphoreType.DMA,
            pltpu.SemaphoreType.DMA((15,)),
            pltpu.SemaphoreType.DMA,
            pltpu.SemaphoreType.DMA((tiles, 6)),
            pltpu.SemaphoreType.DMA((tiles, 12)),
            pltpu.SemaphoreType.DMA((half, tiles)),
            pltpu.SemaphoreType.DMA((half, tiles)),
            pltpu.SemaphoreType.DMA((half, tiles)),
        ],
        compiler_params=pltpu.CompilerParams(
            collective_id=0, has_side_effects=True, vmem_limit_bytes=56 * 2**20),
        name="correct",
    )(proj, dht, nbr.T)
    return (own + theirs.astype(f32)).reshape(rows, half * BT)


def solution(mesh):
    placed = (P("atom", None, "row"), P("atom", "row"), P("atom", None, None, None))
    return jax.shard_map(
        on_device, mesh=mesh, in_specs=placed, out_specs=P("row", ("col", "atom")), check_vma=False
    )
```
